32 devices in a mesh: groups: 2 (over y), wide: 4 (over x, core), narrow: 4 (over z).
Axes of the slice: x: 2, y: 2, z: 4, core: 2. Of those that a mesh axis runs over, the one named last changes fastest.
Arguments:
- hidden_in: bfloat16 [2, 64, 16384], P(None, ('groups', 'wide'), 'narrow'), parts along dimension 1, may hold values from -400 to 400
- norm_gain: bfloat16 [16384], P('narrow'), may hold values from 0.5 to 1.5
- qkv_weight: bfloat16 [16384, 9216], P('narrow', 'wide'), may hold values from -0.046875 to 0.046875
- out_weight: bfloat16 [8192, 16384], P('wide', 'narrow'), may hold values from -0.0625 to 0.0625
- lengths: int32 [64], P(('groups', 'wide', 'narrow')), parts along dimension 0, may hold values from 1 to 2048, as said below
- key_cache: bfloat16 [64, 4, 2048, 128], P(('groups', 'wide', 'narrow')), parts along dimension 0, may hold values from -330 to 330
- cache_of_values: bfloat16 [64, 4, 2048, 128], P(('groups', 'wide', 'narrow')), parts along dimension 0, may hold values from -6 to 6
Outputs:
- block_out: bfloat16 [2, 64, 16384], P(None, ('groups', 'wide'), 'narrow'), parts along dimension 1
The draws below stay inside these ranges and needn't reach their ends.
There are 2 independent parts, one for each index of `groups`. The reference program is written for one: setup_inputs(seed, part) draws one part's arguments, and reference() takes and returns one part's arrays. A program takes and returns all parts, laid end to end along the dimension named above; an argument that names none is the same for every part. Nothing has to cross between parts.
Inputs may be any that keep to these rules, and one draw needn't show every extreme that they name: Sequence r has cache slots 0 to lengths[r] - 1 filled; some sequence of every draw has all 2048 filled.
All inputs are finite; a program needn't handle non-finite values.
Results may differ from the reference program's by a relative error of at most 0.012.
Values may be sent and summed in bfloat16 or wider, within the bound.
No kernel may reach another device: no remote copies, remote signals or barrier semaphores. Data moves between devices by JAX's collectives and lax.ppermute only.
A program may use at most 128 MiB of HBM per device.

```python
import math
import jax
import jax.numpy as jnp
from jax import lax

D = 16384
QUERY_HEADS = 64
KEY_VALUE_HEADS = 4
HEAD_SIZE = 128
DECODE_STEPS = 2
CACHE_SLOTS = 2048
BATCH_ROWS = 32
QKVW = 9216


def length_values(key):
    key = jax.random.fold_in(key, 11)
    keys_list = jax.random.split(key, 5)
    top_bits = CACHE_SLOTS.bit_length() - 1
    exponent = jax.random.randint(keys_list[0], (BATCH_ROWS,), 0, top_bits + 1)
    reach = jnp.left_shift(jnp.ones((BATCH_ROWS,), jnp.int32), exponent.astype(jnp.int32))
    short = jax.random.randint(keys_list[1], (BATCH_ROWS,), 0, reach) + 1
    broad = jax.random.randint(keys_list[2], (BATCH_ROWS,), 1, CACHE_SLOTS + 1)
    picked = jax.random.randint(keys_list[3], (BATCH_ROWS,), 0, 2)
    chosen = jnp.where(picked == 1, broad, short)
    fullest = jax.random.randint(keys_list[4], (), 0, BATCH_ROWS)
    chosen = jnp.where(jnp.arange(BATCH_ROWS) == fullest, CACHE_SLOTS, chosen)
    return chosen.astype(jnp.int32)


def draw_lengths(key, part):
    return length_values(key)


def draw_hidden_in(key, part):
    key = jax.random.fold_in(key, 37)
    first_key = jax.random.fold_in(key, 0)
    key_second = jax.random.fold_in(key, 1)
    key_fourth = jax.random.fold_in(key, 3)
    target_shape = (DECODE_STEPS, BATCH_ROWS, D)
    column_scale = 10.0 ** (jnp.arange(D, dtype=jnp.float32) / D)
    row_scale = jnp.exp(jax.random.uniform(key_second, (DECODE_STEPS, BATCH_ROWS, 1), jnp.float32, 0.0, math.log(10.0)))
    block_exponent = jax.random.uniform(key_fourth, (DECODE_STEPS, BATCH_ROWS, 16, 1), jnp.float32, 0.0, 1.0)
    block_scale = jnp.broadcast_to(10.0 ** (-block_exponent), (DECODE_STEPS, BATCH_ROWS, 16, D // 16)).reshape(target_shape)
    core = jnp.clip(jax.random.normal(first_key, target_shape, jnp.float32), -4.0, 4.0)
    return (core * row_scale * column_scale * block_scale).astype(jnp.bfloat16)


def draw_key_cache(key, part):
    key = jax.random.fold_in(key, 23)
    first_key = jax.random.fold_in(key, 0)
    target_shape = (BATCH_ROWS, KEY_VALUE_HEADS, CACHE_SLOTS, HEAD_SIZE)
    drawn = jnp.clip(jax.random.normal(first_key, target_shape, jnp.float32), -6.0, 6.0)
    return drawn.astype(jnp.bfloat16)


def shard_levels(key, dims, shards, smallest, high):
    level = 1.0
    for axis_at, parts in shards:
        draws = jax.random.uniform(jax.random.fold_in(jax.random.fold_in(key, 6), axis_at), (parts,), jnp.float32, smallest / len(shards), high / len(shards))
        level = level * jnp.repeat(jnp.exp(draws), dims[axis_at] // parts).reshape((-1,) + (1,) * (len(dims) - 1 - axis_at))
    return level


def normal_values(key, dims, width, most, cuts=(), held_as=jnp.bfloat16):
    result = width * jax.random.normal(key, dims, jnp.float32)
    if cuts:
        result = result * shard_levels(key, dims, cuts, -0.22, 0.18)
    return jnp.clip(result, -most, most).astype(held_as)


def setup_inputs(seed: int = 0, part: int = 0) -> dict:
    streams_of = jax.random.split(jax.random.key(seed), 8)
    part_splits = jax.random.split(jax.random.fold_in(streams_of[7], part), 8)
    return {
        "hidden_in": draw_hidden_in(jax.random.fold_in(jax.random.fold_in(streams_of[7], part), 71), part),
        "norm_gain": jnp.clip(1.0 + 0.1 * jax.random.normal(streams_of[1], (D,), jnp.float32), 0.5, 1.5).astype(jnp.bfloat16),
        "qkv_weight": normal_values(streams_of[2], (D, QKVW), D ** -0.5, 0.046875, ((0, 4), (1, 4))),
        "out_weight": normal_values(streams_of[3], (QUERY_HEADS * HEAD_SIZE, D), (QUERY_HEADS * HEAD_SIZE) ** -0.5, 0.0625, ((0, 4), (1, 4))),
        "lengths": draw_lengths(jax.random.fold_in(jax.random.fold_in(streams_of[7], part), 71), part),
        "key_cache": draw_key_cache(jax.random.fold_in(jax.random.fold_in(streams_of[7], part), 71), part),
        "cache_of_values": normal_values(part_splits[6], (BATCH_ROWS, KEY_VALUE_HEADS, CACHE_SLOTS, HEAD_SIZE), 1.0, 6.0, ((0, 16),)),
    }


norm_epsilon = 1e-05
rope_base = 500000.0

def rope_angles(positions, head_dim):
    half = head_dim // 2
    freqs = rope_base ** (-(jnp.arange(half, dtype=jnp.float32) * 2.0 / head_dim))
    angles = positions.astype(jnp.float32)[..., None] * freqs
    return (jnp.cos(angles), jnp.sin(angles))

def rotate(vectors, cosine, sine):
    half = vectors.shape[-1] // 2
    first = vectors[..., :half]
    second = vectors[..., half:]
    cosine = cosine[..., None, :]
    sine = sine[..., None, :]
    return jnp.concatenate([first * cosine - second * sine, second * cosine + first * sine], axis=-1)

def reference(hidden_in, norm_gain, qkv_weight, out_weight, lengths, key_cache, cache_of_values):
    hidden = hidden_in.astype(jnp.float32)
    mean_square = lax.optimization_barrier(jnp.mean(hidden * hidden, axis=-1, keepdims=True))
    normed = (hidden * lax.rsqrt(mean_square + norm_epsilon) * norm_gain.astype(jnp.float32)).astype(jnp.bfloat16)
    projected_rows = jnp.dot(normed.reshape(DECODE_STEPS * BATCH_ROWS, D), qkv_weight, preferred_element_type=jnp.float32)
    projected_rows = projected_rows.astype(jnp.bfloat16).reshape(DECODE_STEPS, BATCH_ROWS, QKVW)
    width_query = QUERY_HEADS * HEAD_SIZE
    key_value_width = KEY_VALUE_HEADS * HEAD_SIZE
    head_group = QUERY_HEADS // KEY_VALUE_HEADS
    query_rows = projected_rows[..., :width_query].astype(jnp.float32).reshape(DECODE_STEPS, BATCH_ROWS, QUERY_HEADS, HEAD_SIZE)
    incoming_keys = projected_rows[..., width_query:width_query + key_value_width].astype(jnp.float32).reshape(DECODE_STEPS, BATCH_ROWS, KEY_VALUE_HEADS, HEAD_SIZE)
    incoming_values = projected_rows[..., width_query + key_value_width:].reshape(DECODE_STEPS, BATCH_ROWS, KEY_VALUE_HEADS, HEAD_SIZE)
    positions = lengths[None, :] + jnp.arange(DECODE_STEPS, dtype=jnp.int32)[:, None]
    cosine, sine = rope_angles(positions, HEAD_SIZE)
    query_rows = rotate(query_rows, cosine, sine).astype(jnp.bfloat16)
    incoming_keys = rotate(incoming_keys, cosine, sine).astype(jnp.bfloat16)
    query_rows, incoming_keys = lax.optimization_barrier((query_rows, incoming_keys))
    cache_keys = key_cache.astype(jnp.float32)
    cache_values = cache_of_values.astype(jnp.float32)
    valid = jnp.arange(CACHE_SLOTS, dtype=jnp.int32)[None, :] < lengths[:, None]
    scale = HEAD_SIZE ** (-0.5)
    outputs = []
    for decode_step in range(DECODE_STEPS):
        grouped_heads = query_rows[decode_step].astype(jnp.float32).reshape(BATCH_ROWS, KEY_VALUE_HEADS, head_group, HEAD_SIZE)
        cached = jnp.einsum('rkgd,rkcd->rkgc', grouped_heads, cache_keys) * scale
        cached = jnp.where(valid[:, None, None, :], cached, -jnp.inf)
        fresh_keys = incoming_keys[:decode_step + 1].astype(jnp.float32)
        fresh_values = incoming_values[:decode_step + 1].astype(jnp.float32)
        fresh = jnp.einsum('rkgd,jrkd->rkgj', grouped_heads, fresh_keys) * scale
        highest = jnp.maximum(lax.optimization_barrier(jnp.max(cached, axis=-1)), lax.optimization_barrier(jnp.max(fresh, axis=-1)))
        weights_cache = jnp.exp(cached - highest[..., None])
        weights_new = jnp.exp(fresh - highest[..., None])
        denominator = lax.optimization_barrier(jnp.sum(weights_cache, axis=-1)) + lax.optimization_barrier(jnp.sum(weights_new, axis=-1))
        rounded_cache = lax.optimization_barrier(weights_cache.astype(jnp.bfloat16)).astype(jnp.float32)
        rounded_new = lax.optimization_barrier(weights_new.astype(jnp.bfloat16)).astype(jnp.float32)
        totals = jnp.einsum('rkgc,rkcd->rkgd', rounded_cache, cache_values)
        totals = totals + jnp.einsum('rkgj,jrkd->rkgd', rounded_new, fresh_values)
        outputs.append((totals / denominator[..., None]).astype(jnp.bfloat16).reshape(BATCH_ROWS, width_query))
    attended = jnp.stack(outputs)
    block_out = jnp.dot(attended.reshape(DECODE_STEPS * BATCH_ROWS, width_query), out_weight, preferred_element_type=jnp.float32)
    return block_out.astype(jnp.bfloat16).reshape(DECODE_STEPS, BATCH_ROWS, D)
```

```python
import functools

import jax
import jax.numpy as jnp
import numpy as np
from jax import lax
from jax.experimental import pallas as pl
from jax.experimental.pallas import tpu as pltpu
from jax.sharding import PartitionSpec as P

F32 = jnp.float32
BF16 = jnp.bfloat16
LANES = 128
MIB = 1 << 20
norm_epsilon = 1e-05
rope_base = 500000.0


def row_order(tokens, steps, narrow, rows, owner_major):
    out = lax.broadcasted_iota(jnp.int32, (tokens, tokens), 0)
    src = lax.broadcasted_iota(jnp.int32, (tokens, tokens), 1)
    block = steps * narrow * rows
    row = lax.rem(out, rows)
    inner = lax.div(lax.rem(out, block), rows)
    if owner_major:
        step, owner = lax.rem(inner, steps), lax.div(inner, steps)
        want = (step * narrow + owner) * rows + row
    else:
        owner, step = lax.rem(inner, narrow), lax.div(inner, narrow)
        want = (owner * steps + step) * rows + row
    want = want + lax.div(out, block) * block
    return (src == want).astype(BF16)


def chunks(total, size):
    return [(at, min(size, total - at)) for at in range(0, total, size)]


def project_kernel(steps, narrow, rows, x_ref, gain_ref, w_ref, o_ref, scaled):
    tokens, depth = x_ref.shape
    width = w_ref.shape[1]
    per = steps * rows
    order = row_order(tokens, steps, narrow, rows, True)
    squares = jnp.zeros((tokens, 1), F32)
    for at, size in chunks(depth, 512):
        part = jnp.dot(order, x_ref[:, at : at + size], preferred_element_type=F32)
        squares = squares + jnp.sum(part * part, axis=1, keepdims=True)
        scaled[:, at : at + size] = (part * gain_ref[:, at : at + size].astype(F32)).astype(BF16)
    high = squares.astype(BF16).astype(F32)
    lane = lax.broadcasted_iota(jnp.int32, (tokens, LANES), 1)
    head = jnp.where(lane == 0, high, jnp.where(lane == 1, squares - high, 0.0)).astype(BF16)
    for d in range(tokens // per):
        o_ref[d, :, :LANES] = head[d * per : (d + 1) * per]
    for at, size in chunks(width, 768):
        y = jnp.dot(scaled[...], w_ref[:, at : at + size], preferred_element_type=F32).astype(BF16)
        for d in range(tokens // per):
            o_ref[d, :, LANES + at : LANES + at + size] = y[d * per : (d + 1) * per]


def attend_kernel(
    wide, narrow, steps, model, slice_width,
    lengths_ref, part_ref, cos_ref, sin_ref, key_ref, value_ref, o_ref, proj, query, total,
):
    rows, kv_heads, slots, head_dim = key_ref.shape
    per = steps * rows
    width = part_ref.shape[2] - LANES
    width_query = slice_width * wide
    heads = width_query // head_dim
    group = heads // kv_heads
    scale = head_dim ** (-0.5)

    head = part_ref[0:narrow, :, 0:LANES].astype(F32)
    head = jnp.sum(head, axis=0)
    squares = head[:, 0:1] + head[:, 1:2]
    factor = lax.rsqrt(squares / model + norm_epsilon)
    for w in range(wide):
        part = part_ref[w * narrow, :, LANES:].astype(F32)
        for n in range(1, narrow):
            part = part + part_ref[w * narrow + n, :, LANES:].astype(F32)
        proj[:, w * width : (w + 1) * width] = (part * factor).astype(BF16).astype(F32)

    cosine = cos_ref[...]
    sine = sin_ref[...]

    def turned(at):
        x = proj[:, at : at + head_dim]
        return (x * cosine + pltpu.roll(x, head_dim // 2, 1) * sine).astype(BF16).astype(F32)

    for h in range(heads):
        q = turned(h * head_dim)
        for s in range(steps):
            for r in range(rows):
                i = s * rows + r
                query[h // group, r, s * group + h % group : s * group + h % group + 1, :] = q[i : i + 1]
    lane = lax.broadcasted_iota(jnp.int32, (steps * group, slots), 1)
    sub = lax.broadcasted_iota(jnp.int32, (steps * group, 1), 0)
    step_of = lax.div(sub, group)
    for k in range(kv_heads):
        fresh_key = turned(width_query + k * head_dim)
        at = width_query + (kv_heads + k) * head_dim
        fresh_value = proj[:, at : at + head_dim]
        for r in range(rows):
            q = query[k, r]
            scores = lax.dot_general(
                q.astype(BF16), key_ref[r, k], (((1,), (1,)), ((), ())), preferred_element_type=F32
            ) * scale
            scores = jnp.where(lane < lengths_ref[r], scores, -jnp.inf)
            highest = jnp.max(scores, axis=1, keepdims=True)
            newest = []
            for j in range(steps):
                i = j * rows + r
                dot = jnp.sum(q * fresh_key[i : i + 1], axis=1, keepdims=True) * scale
                dot = jnp.where(step_of >= j, dot, -jnp.inf)
                newest.append(dot)
                highest = jnp.maximum(highest, dot)
            weights = jnp.exp(scores - highest)
            denominator = jnp.sum(weights, axis=1, keepdims=True)
            out = jnp.dot(weights.astype(BF16), value_ref[r, k], preferred_element_type=F32)
            for j in range(steps):
                i = j * rows + r
                weight = jnp.exp(newest[j] - highest)
                denominator = denominator + weight
                out = out + weight.astype(BF16).astype(F32) * fresh_value[i : i + 1]
            out = out / denominator
            for s in range(steps):
                for g in range(group):
                    at = (k * group + g) * head_dim
                    w, col = at // slice_width, at % slice_width
                    total[w, s * rows + r : s * rows + r + 1, col : col + head_dim] = out[
                        s * group + g : s * group + g + 1
                    ]
    for w in range(wide):
        message = total[w].astype(BF16)
        for n in range(narrow):
            o_ref[w * narrow + n] = message


def output_kernel(steps, narrow, rows, x_ref, w_ref, o_ref, gathered, ordered):
    sources, per, depth = x_ref.shape
    tokens = sources * per
    for d in range(sources):
        gathered[d * per : (d + 1) * per] = x_ref[d].astype(F32)
    order = row_order(tokens, steps, narrow, rows, False)
    for at, size in chunks(depth, 512):
        ordered[:, at : at + size] = jnp.dot(
            order, gathered[:, at : at + size].astype(BF16), preferred_element_type=F32
        ).astype(BF16)
    for at, size in chunks(w_ref.shape[1], 512):
        o_ref[:, at : at + size] = jnp.dot(
            ordered[...], w_ref[:, at : at + size], preferred_element_type=F32
        ).astype(BF16)


def whole():
    return pl.BlockSpec(memory_space=pltpu.VMEM)


def resident(array):
    return pltpu.with_memory_space_constraint(array, pltpu.VMEM)


def body(hidden_in, norm_gain, qkv_weight, out_weight, lengths, key_cache, cache_of_values):
    wide = lax.axis_size("wide")
    narrow = lax.axis_size("narrow")
    steps, block_rows, depth = hidden_in.shape
    rows, kv_heads, slots, head_dim = key_cache.shape
    width = qkv_weight.shape[1]
    slice_width, out_width = out_weight.shape
    tokens = steps * block_rows * wide
    sources = wide * narrow
    per = steps * rows
    heads = slice_width * wide // head_dim

    with jax.named_scope("rotary_angles"):
        positions = (lengths[None, :] + jnp.arange(steps, dtype=jnp.int32)[:, None]).reshape(-1)
        half = head_dim // 2
        freqs = rope_base ** (-(jnp.arange(half, dtype=F32) * 2.0 / head_dim))
        angles = positions.astype(F32)[:, None] * freqs
        cosine = jnp.concatenate([jnp.cos(angles), jnp.cos(angles)], axis=1)
        sine = jnp.concatenate([-jnp.sin(angles), jnp.sin(angles)], axis=1)

    gathered = lax.all_gather(hidden_in.reshape(steps * block_rows, depth), "wide", axis=0, tiled=True)
    partial = pl.pallas_call(
        functools.partial(project_kernel, steps, narrow, rows),
        out_shape=jax.ShapeDtypeStruct((sources, per, LANES + width), BF16),
        in_specs=[whole()] * 3,
        out_specs=whole(),
        scratch_shapes=[pltpu.VMEM((tokens, depth), BF16)],
        compiler_params=pltpu.CompilerParams(vmem_limit_bytes=12 * MIB),
        cost_estimate=pl.CostEstimate(
            flops=2 * tokens * depth * width, bytes_accessed=2 * depth * width, transcendentals=0
        ),
        name="project",
    )(gathered, norm_gain.reshape(1, -1), resident(qkv_weight))
    parts = lax.all_to_all(partial, ("wide", "narrow"), 0, 0, tiled=True)
    attended = pl.pallas_call(
        functools.partial(attend_kernel, wide, narrow, steps, depth * narrow, slice_width),
        out_shape=jax.ShapeDtypeStruct((sources, per, slice_width), BF16),
        in_specs=[pl.BlockSpec(memory_space=pltpu.SMEM)] + [whole()] * 5,
        out_specs=whole(),
        scratch_shapes=[
            pltpu.VMEM((per, width * wide), F32),
            pltpu.VMEM((kv_heads, rows, steps * heads // kv_heads, head_dim), F32),
            pltpu.VMEM((wide, per, slice_width), F32),
        ],
        compiler_params=pltpu.CompilerParams(vmem_limit_bytes=12 * MIB),
        cost_estimate=pl.CostEstimate(
            flops=4 * per * heads * slots * head_dim,
            bytes_accessed=4 * rows * kv_heads * slots * head_dim,
            transcendentals=per * heads * slots,
        ),
        name="attend",
    )(lengths, parts, cosine, sine, resident(key_cache), resident(cache_of_values))
    spread = lax.all_to_all(attended, ("wide", "narrow"), 0, 0, tiled=True)
    products = pl.pallas_call(
        functools.partial(output_kernel, steps, narrow, rows),
        out_shape=jax.ShapeDtypeStruct((tokens, out_width), BF16),
        in_specs=[whole()] * 2,
        out_specs=whole(),
        scratch_shapes=[pltpu.VMEM((tokens, slice_width), F32), pltpu.VMEM((tokens, slice_width), BF16)],
        compiler_params=pltpu.CompilerParams(vmem_limit_bytes=12 * MIB),
        cost_estimate=pl.CostEstimate(
            flops=2 * tokens * slice_width * out_width, bytes_accessed=2 * slice_width * out_width, transcendentals=0
        ),
        name="output",
    )(spread, resident(out_weight))
    sums = lax.all_to_all(products.reshape(wide, steps * block_rows, out_width), "wide", 0, 0, tiled=True)
    total = jnp.sum(sums.astype(F32), axis=0).astype(BF16)
    return total.reshape(steps, block_rows, out_width)


def solution(mesh):
    in_specs = (
        P(None, ("groups", "wide"), "narrow"),
        P("narrow"),
        P("narrow", "wide"),
        P("wide", "narrow"),
        P(("groups", "wide", "narrow")),
        P(("groups", "wide", "narrow"), None, None, None),
        P(("groups", "wide", "narrow"), None, None, None),
    )
    out_specs = P(None, ("groups", "wide"), "narrow")
    return jax.shard_map(body, mesh=mesh, in_specs=in_specs, out_specs=out_specs, check_vma=False)
```

```python
import functools

import jax
import jax.numpy as jnp
import numpy as np
from jax import lax
from jax.experimental import pallas as pl
from jax.experimental.pallas import tpu as pltpu
from jax.sharding import PartitionSpec as P

F32 = jnp.float32
BF16 = jnp.bfloat16
LANES = 128
MIB = 1 << 20
norm_epsilon = 1e-05
rope_base = 500000.0


def chunks(total, size):
    return [(at, min(size, total - at)) for at in range(0, total, size)]


def iotas(tokens):
    out = lax.broadcasted_iota(jnp.int32, (tokens, tokens), 0)
    src = lax.broadcasted_iota(jnp.int32, (tokens, tokens), 1)
    return out, src


def whole():
    return pl.BlockSpec(memory_space=pltpu.VMEM)


def hbm():
    return pl.BlockSpec(memory_space=pl.ANY)


def params():
    return pltpu.CompilerParams(vmem_limit_bytes=16 * MIB)


def swap(array, axis, distance):
    size = lax.axis_size(axis)
    return lax.ppermute(array, axis, [(i, i ^ distance) for i in range(size)])


def resident(array):
    return pltpu.with_memory_space_constraint(array, pltpu.VMEM)


def fetch_kernel(spans, turns, *refs):
    count = len(spans)
    sources, sem = refs[:count], refs[-1]
    outs = refs[len(refs) - 1 - count - 2 * bool(turns) : -1]
    copies = []
    for i, (at, size) in enumerate(spans):
        copies.append(pltpu.make_async_copy(sources[i].at[pl.ds(at, size)], outs[i], sem.at[i]))
    for copy in copies:
        copy.start()
    if turns:
        steps, rows = turns
        lengths_ref, freqs_ref = refs[count : count + 2]
        cos_ref, sin_ref = outs[-2:]
        for s in range(steps):
            for r in range(rows):
                i = s * rows + r
                angle = (lengths_ref[r] + s).astype(F32) * freqs_ref[...]
                lane = lax.broadcasted_iota(jnp.int32, angle.shape, 1)
                cos_ref[i : i + 1] = jnp.cos(angle)
                sin_ref[i : i + 1] = jnp.where(lane < angle.shape[1] // 2, -1.0, 1.0) * jnp.sin(angle)
    for copy in copies:
        copy.wait()


def fetch(spans, after, turns=()):
    arrays = [pltpu.with_memory_space_constraint(a, pltpu.HBM) for a, _, _ in spans]
    outs = [pltpu.VMEM((n,) + a.shape[1:], a.dtype) for a, _, n in spans]
    size = sum(2 * n * a.size // a.shape[0] * a.dtype.itemsize for a, _, n in spans)
    extra, extra_specs = [], []
    if turns:
        steps, lengths, freqs = turns
        turns = (steps, lengths.shape[0])
        extra, extra_specs = [lengths, freqs], [pl.BlockSpec(memory_space=pltpu.SMEM), whole()]
        outs += [jax.ShapeDtypeStruct((steps * lengths.shape[0], freqs.shape[1]), F32)] * 2
    return pl.pallas_call(
        functools.partial(fetch_kernel, [(at, n) for _, at, n in spans], turns),
        out_shape=outs,
        in_specs=[pl.BlockSpec(memory_space=pltpu.HBM)] * len(arrays) + extra_specs + [hbm()] * len(after),
        out_specs=[whole()] * len(outs),
        scratch_shapes=[pltpu.SemaphoreType.DMA((len(arrays),))],
        compiler_params=params(),
        cost_estimate=pl.CostEstimate(flops=0, bytes_accessed=size, transcendentals=0),
        name="fetch",
    )(*arrays, *extra, *after)


def project_kernel(wide, narrow, steps, rows, *refs):
    blocks, (gain_ref, near_ref, w_ref) = refs[:wide], refs[wide : wide + 3]
    outs, (scaled, acc, far, sem) = refs[wide + 3 : -4], refs[-4:]
    block, depth = blocks[0].shape
    tokens = block * wide
    split, width = near_ref.shape
    rest = []
    for i, (at, size) in enumerate(chunks(depth - split, 512)):
        rest.append(
            pltpu.make_async_copy(w_ref.at[pl.ds(split + at, size)], far.at[pl.ds(at, size)], sem.at[i])
        )
        rest[-1].start()
    per = steps * rows
    here = lax.axis_index("narrow")
    out, src = iotas(tokens)
    row = lax.rem(out, rows)
    step = lax.rem(lax.div(out, rows), steps)
    d = lax.rem(lax.div(out, per), wide)
    owner = lax.bitwise_xor(lax.div(out, per * wide), here)
    order = (src == ((d * steps + step) * narrow + owner) * rows + row).astype(BF16)
    squares = jnp.zeros((tokens, 1), F32)
    for at, size in chunks(depth, 512):
        x = jnp.concatenate([b[:, at : at + size] for b in blocks], axis=0)
        part = jnp.dot(order, x, preferred_element_type=F32)
        squares = squares + jnp.sum(part * part, axis=1, keepdims=True)
        scaled[:, at : at + size] = (part * gain_ref[:, at : at + size].astype(F32)).astype(BF16)
    high = squares.astype(BF16).astype(F32)
    lane = lax.broadcasted_iota(jnp.int32, (tokens, LANES), 1)
    head = jnp.where(lane == 0, high, jnp.where(lane == 1, squares - high, 0.0)).astype(BF16)
    span = per * wide
    for e in range(narrow):
        outs[e][:, :LANES] = head[e * span : (e + 1) * span]
    for at, size in chunks(width, 768):
        acc[:, at : at + size] = jnp.dot(
            scaled[:, :split], near_ref[:, at : at + size], preferred_element_type=F32
        )
    for i, (low, deep) in enumerate(chunks(depth - split, 512)):
        rest[i].wait()
        for at, size in chunks(width, 768):
            y = acc[:, at : at + size] + jnp.dot(
                scaled[:, split + low : split + low + deep],
                far[low : low + deep, at : at + size],
                preferred_element_type=F32,
            )
            if i < len(rest) - 1:
                acc[:, at : at + size] = y
                continue
            y = y.astype(BF16)
            for e in range(narrow):
                outs[e][:, LANES + at : LANES + at + size] = y[e * span : (e + 1) * span]


def normalize_kernel(wide, narrow, model, *refs):
    parts, outs = refs[:narrow], refs[-wide:]
    per = outs[0].shape[0]
    head = sum(p[:, :LANES].astype(F32) for p in parts)
    factor = lax.rsqrt((head[:, 0:1] + head[:, 1:2]) / model + norm_epsilon)
    total = sum(p[:, LANES:].astype(F32) for p in parts) * factor
    for d in range(wide):
        outs[d][...] = total[d * per : (d + 1) * per].astype(BF16)


def attend_kernel(wide, steps, slice_width, *refs):
    lengths_ref, parts = refs[0], refs[1 : 1 + wide]
    cos_ref, sin_ref, key_ref, value_ref = refs[1 + wide : 5 + wide]
    outs = refs[5 + wide : 5 + 2 * wide]
    stack, proj, query, total = refs[5 + 2 * wide :]
    rows, kv_heads, slots, head_dim = key_ref.shape
    width = parts[0].shape[1]
    width_query = slice_width * wide
    heads = width_query // head_dim
    group = heads // kv_heads
    scale = head_dim ** (-0.5)
    here = lax.axis_index("wide")

    for d in range(wide):
        stack[d] = parts[d][...].astype(F32)
    for w in range(wide):
        proj[:, w * width : (w + 1) * width] = stack[lax.bitwise_xor(here, w)]

    cosine = cos_ref[...]
    sine = sin_ref[...]

    def turned(at):
        x = proj[:, at : at + head_dim]
        return (x * cosine + pltpu.roll(x, head_dim // 2, 1) * sine).astype(BF16).astype(F32)

    for h in range(heads):
        q = turned(h * head_dim)
        for s in range(steps):
            for r in range(rows):
                i = s * rows + r
                at = s * group + h % group
                query[h // group, r, at : at + 1, :] = q[i : i + 1]
    lane = lax.broadcasted_iota(jnp.int32, (steps * group, slots), 1)
    step_of = lax.div(lax.broadcasted_iota(jnp.int32, (steps * group, 1), 0), group)
    for k in range(kv_heads):
        fresh_key = turned(width_query + k * head_dim)
        at = width_query + (kv_heads + k) * head_dim
        fresh_value = proj[:, at : at + head_dim]
        for r in range(rows):
            q = query[k, r]
            scores = lax.dot_general(
                q.astype(BF16), key_ref[r, k], (((1,), (1,)), ((), ())), preferred_element_type=F32
            ) * scale
            scores = jnp.where(lane < lengths_ref[r], scores, -jnp.inf)
            highest = jnp.max(scores, axis=1, keepdims=True)
            newest = []
            for j in range(steps):
                i = j * rows + r
                dot = jnp.sum(q * fresh_key[i : i + 1], axis=1, keepdims=True) * scale
                dot = jnp.where(step_of >= j, dot, -jnp.inf)
                newest.append(dot)
                highest = jnp.maximum(highest, dot)
            weights = jnp.exp(scores - highest)
            denominator = jnp.sum(weights, axis=1, keepdims=True)
            out = jnp.dot(weights.astype(BF16), value_ref[r, k], preferred_element_type=F32)
            for j in range(steps):
                i = j * rows + r
                weight = jnp.exp(newest[j] - highest)
                denominator = denominator + weight
                out = out + weight.astype(BF16).astype(F32) * fresh_value[i : i + 1]
            out = out / denominator
            for s in range(steps):
                for g in range(group):
                    at = (k * group + g) * head_dim
                    w, col = at // slice_width, at % slice_width
                    i = s * rows + r
                    total[w, i : i + 1, col : col + head_dim] = out[s * group + g : s * group + g + 1]
    for d in range(wide):
        outs[d][...] = total[lax.bitwise_xor(here, d)].astype(BF16)


def join_kernel(*refs):
    per = refs[0].shape[0]
    scratch = refs[-1]
    for d, ref in enumerate(refs[:-2]):
        scratch[d * per : (d + 1) * per] = ref[...].astype(F32)
    refs[-2][...] = scratch[...].astype(BF16)


def output_kernel(wide, narrow, steps, rows, *refs):
    blocks, w_refs, (keep_ref, send_ref, ordered) = refs[:narrow], refs[narrow:-3], refs[-3:]
    split = w_refs[0].shape[0]
    block, depth = blocks[0].shape
    tokens = block * narrow
    per = steps * rows
    here = lax.axis_index("narrow")
    out, src = iotas(tokens)
    row = lax.rem(out, rows)
    owner = lax.rem(lax.div(out, rows), narrow)
    step = lax.rem(lax.div(out, rows * narrow), steps)
    d = lax.div(out, per * narrow)
    d = lax.rem(d, wide // 2) * 2 + lax.div(d, wide // 2)
    e = lax.bitwise_xor(owner, here)
    order = (src == ((e * wide + d) * steps + step) * rows + row).astype(BF16)
    for at, size in chunks(depth, 512):
        x = jnp.concatenate([b[:, at : at + size] for b in blocks], axis=0)
        ordered[:, at : at + size] = jnp.dot(order, x, preferred_element_type=F32).astype(BF16)
    half = tokens // 2
    for at, size in chunks(w_refs[0].shape[1], 512):
        y = jnp.dot(ordered[:, :split], w_refs[0][:, at : at + size], preferred_element_type=F32)
        y = y + jnp.dot(ordered[:, split:], w_refs[1][:, at : at + size], preferred_element_type=F32)
        keep_ref[:, at : at + size] = y[:half]
        send_ref[:, at : at + size] = y[half:].astype(BF16)


def pair_kernel(keep_ref, other_ref, *outs):
    block = outs[0].shape[0]
    for x, out in enumerate(outs):
        span = pl.ds(x * block, block)
        out[...] = (keep_ref[span] + other_ref[span].astype(F32)).astype(out.dtype)


def total_kernel(*refs):
    refs[-1][...] = sum(ref[...].astype(F32) for ref in refs[:-1]).astype(BF16)


def call(kernel, name, outs, inputs, scratch=(), specs=None, flops=0, size=0, exps=0):
    return pl.pallas_call(
        kernel,
        out_shape=outs,
        in_specs=specs or [whole()] * len(inputs),
        out_specs=jax.tree.map(lambda _: whole(), outs),
        scratch_shapes=list(scratch),
        compiler_params=params(),
        cost_estimate=pl.CostEstimate(flops=flops, bytes_accessed=size, transcendentals=exps),
        name=name,
    )(*inputs)


def body(hidden_in, norm_gain, qkv_weight, out_weight, lengths, key_cache, cache_of_values):
    wide = lax.axis_size("wide")
    narrow = lax.axis_size("narrow")
    steps, block_rows, depth = hidden_in.shape
    rows, kv_heads, slots, head_dim = key_cache.shape
    width = qkv_weight.shape[1]
    slice_width, out_width = out_weight.shape
    block = steps * block_rows
    tokens = block * wide
    per = steps * rows
    heads = slice_width * wide // head_dim
    shape = jax.ShapeDtypeStruct

    half = np.arange(head_dim) % (head_dim // 2)
    freqs = np.asarray(rope_base ** (-2.0 * half / head_dim), np.float32)[None]
    qkv_split = depth // 2
    out_split = slice_width // 2

    (qkv_near,) = fetch([(qkv_weight, 0, qkv_split)], [])
    with jax.named_scope("gather_tokens"):
        own = hidden_in.reshape(block, depth)
        blocks = []
        for x in range(wide // 2):
            near = swap(own, "wide", 2 * x) if x else own
            if x:
                near, qkv_near = lax.optimization_barrier((near, qkv_near))
            blocks += [near, swap(near, "wide", 1)]
    partial = call(
        functools.partial(project_kernel, wide, narrow, steps, rows), "project",
        [shape((per * wide, LANES + width), BF16)] * narrow,
        blocks
        + [norm_gain.reshape(1, -1), resident(qkv_near), pltpu.with_memory_space_constraint(qkv_weight, pltpu.HBM)],
        [
            pltpu.VMEM((tokens, depth), BF16),
            pltpu.VMEM((tokens, width), F32),
            pltpu.VMEM((depth - qkv_split, width), BF16),
            pltpu.SemaphoreType.DMA((-(-(depth - qkv_split) // 512),)),
        ],
        [whole()] * (wide + 2) + [pl.BlockSpec(memory_space=pltpu.HBM)],
        flops=2 * tokens * depth * width, size=2 * depth * width,
    )
    keys, values, out_near, cosine, sine = fetch(
        [(key_cache, 0, rows), (cache_of_values, 0, rows), (out_weight, 0, out_split)],
        [partial[0]],
        (steps, lengths, jnp.asarray(freqs)),
    )
    with jax.named_scope("sum_over_narrow"):
        parts = [swap(p, "narrow", e) if e else p for e, p in enumerate(partial)]
    normed = call(
        functools.partial(normalize_kernel, wide, narrow, depth * narrow), "normalize",
        [shape((per, width), BF16)] * wide,
        parts + [cosine],
        specs=[whole()] * narrow + [hbm()],
        size=4 * tokens * width,
    )
    with jax.named_scope("columns_to_owner"):
        mine = [swap(p, "wide", d) if d else p for d, p in enumerate(normed)]
    attended = call(
        functools.partial(attend_kernel, wide, steps, slice_width), "attend",
        [shape((per, slice_width), BF16)] * wide,
        [lengths] + mine + [cosine, sine, resident(keys), resident(values)],
        [
            pltpu.VMEM((wide, per, width), F32),
            pltpu.VMEM((per, width * wide), F32),
            pltpu.VMEM((kv_heads, rows, steps * heads // kv_heads, head_dim), F32),
            pltpu.VMEM((wide, per, slice_width), F32),
        ],
        [pl.BlockSpec(memory_space=pltpu.SMEM)] + [whole()] * (wide + 4),
        flops=4 * per * heads * slots * head_dim,
        size=4 * rows * kv_heads * slots * head_dim,
        exps=per * heads * slots,
    )
    with jax.named_scope("heads_to_weights"):
        arrived = [swap(p, "wide", d) if d else p for d, p in enumerate(attended)]
    joined = call(
        join_kernel, "join", shape((per * wide, slice_width), BF16), arrived,
        [pltpu.VMEM((per * wide, slice_width), F32)], size=4 * per * wide * slice_width,
    )
    (out_far,) = fetch([(out_weight, out_split, slice_width - out_split)], [joined])
    with jax.named_scope("gather_over_narrow"):
        spread = [swap(joined, "narrow", e) if e else joined for e in range(narrow)]
    keep, send = call(
        functools.partial(output_kernel, wide, narrow, steps, rows), "output",
        [shape((tokens // 2, out_width), F32), shape((tokens // 2, out_width), BF16)],
        spread + [resident(out_near), resident(out_far)],
        [pltpu.VMEM((tokens, slice_width), BF16)],
        flops=2 * tokens * slice_width * out_width, size=2 * slice_width * out_width,
    )
    with jax.named_scope("sum_over_wide"):
        other = swap(send, "wide", 1)
        chip = call(
            pair_kernel, "pair",
            [shape((block, out_width), BF16 if x else F32) for x in range(wide // 2)],
            [keep, other], size=6 * tokens * out_width // 2,
        )
        sums = [swap(c, "wide", 2 * x) if x else c for x, c in enumerate(chip)]
    total = call(
        total_kernel, "total", shape((block, out_width), BF16), sums, size=8 * block * out_width
    )
    return total.reshape(steps, block_rows, out_width)


def solution(mesh):
    in_specs = (
        P(None, ("groups", "wide"), "narrow"),
        P("narrow"),
        P("narrow", "wide"),
        P("wide", "narrow"),
        P(("groups", "wide", "narrow")),
        P(("groups", "wide", "narrow"), None, None, None),
        P(("groups", "wide", "narrow"), None, None, None),
    )
    out_specs = P(None, ("groups", "wide"), "narrow")
    return jax.shard_map(body, mesh=mesh, in_specs=in_specs, out_specs=out_specs, check_vma=False)
```

```python
import functools
import math

import jax
import jax.numpy as jnp
import numpy as np
from jax import lax
from jax.experimental import pallas as pl
from jax.experimental.pallas import tpu as pltpu
from jax.sharding import PartitionSpec as P

F32 = jnp.float32
BF16 = jnp.bfloat16
LANES = 128
MIB = 1 << 20
norm_epsilon = 1e-05
rope_base = 500000.0


def chunks(total, size):
    return [(at, min(size, total - at)) for at in range(0, total, size)]


def iotas(tokens):
    out = lax.broadcasted_iota(jnp.int32, (tokens, tokens), 0)
    src = lax.broadcasted_iota(jnp.int32, (tokens, tokens), 1)
    return out, src


def whole():
    return pl.BlockSpec(memory_space=pltpu.VMEM)


def hbm():
    return pl.BlockSpec(memory_space=pl.ANY)


def params():
    return pltpu.CompilerParams(vmem_limit_bytes=16 * MIB)


def swap(array, axis, distance):
    size = lax.axis_size(axis)
    return lax.ppermute(array, axis, [(i, i ^ distance) for i in range(size)])


def resident(array):
    return pltpu.with_memory_space_constraint(array, pltpu.VMEM)


def fetch_kernel(spans, turns, *refs):
    count = len(spans)
    sources, sem = refs[:count], refs[-1]
    outs = refs[len(refs) - 1 - count - 3 * bool(turns) : -1]
    copies = []
    for i, (at, size) in enumerate(spans):
        copies.append(pltpu.make_async_copy(sources[i].at[pl.ds(at, size)], outs[i], sem.at[i]))
    for copy in copies:
        copy.start()
    if turns:
        steps, rows = turns
        lengths_ref, freqs_ref = refs[count : count + 2]
        cos_ref, sin_ref, mask_ref = outs[-3:]
        for s in range(steps):
            for r in range(rows):
                i = s * rows + r
                angle = (lengths_ref[r] + s).astype(F32) * freqs_ref[...]
                lane = lax.broadcasted_iota(jnp.int32, angle.shape, 1)
                cos_ref[i : i + 1] = jnp.cos(angle)
                sin_ref[i : i + 1] = jnp.where(lane < angle.shape[1] // 2, -1.0, 1.0) * jnp.sin(angle)
        slot = lax.broadcasted_iota(jnp.int32, (1, mask_ref.shape[1]), 1)
        for r in range(rows):
            mask_ref[r : r + 1] = jnp.where(slot < lengths_ref[r], 0.0, -jnp.inf)
    for copy in copies:
        copy.wait()


def fetch(spans, after, turns=()):
    arrays = [pltpu.with_memory_space_constraint(a, pltpu.HBM) for a, _, _ in spans]
    outs = [pltpu.VMEM((n,) + a.shape[1:], a.dtype) for a, _, n in spans]
    size = sum(2 * n * a.size // a.shape[0] * a.dtype.itemsize for a, _, n in spans)
    extra, extra_specs = [], []
    if turns:
        steps, lengths, freqs = turns
        turns = (steps, lengths.shape[0])
        extra, extra_specs = [lengths, freqs], [pl.BlockSpec(memory_space=pltpu.SMEM), whole()]
        outs += [jax.ShapeDtypeStruct((steps * lengths.shape[0], freqs.shape[1]), F32)] * 2
        outs += [jax.ShapeDtypeStruct((lengths.shape[0], arrays[0].shape[2]), F32)]
    return pl.pallas_call(
        functools.partial(fetch_kernel, [(at, n) for _, at, n in spans], turns),
        out_shape=outs,
        in_specs=[pl.BlockSpec(memory_space=pltpu.HBM)] * len(arrays) + extra_specs + [hbm()] * len(after),
        out_specs=[whole()] * len(outs),
        scratch_shapes=[pltpu.SemaphoreType.DMA((len(arrays),))],
        compiler_params=params(),
        cost_estimate=pl.CostEstimate(flops=0, bytes_accessed=size, transcendentals=0),
        name="fetch",
    )(*arrays, *extra, *after)


def project_kernel(wide, narrow, steps, rows, *refs):
    blocks, (gain_ref, near_ref, w_ref) = refs[:wide], refs[wide : wide + 3]
    outs, (scaled, acc, far, sem) = refs[wide + 3 : -4], refs[-4:]
    block, depth = blocks[0].shape
    tokens = block * wide
    split, width = near_ref.shape
    rest = []
    for i, (at, size) in enumerate(chunks(depth - split, 512)):
        rest.append(
            pltpu.make_async_copy(w_ref.at[pl.ds(split + at, size)], far.at[pl.ds(at, size)], sem.at[i])
        )
        rest[-1].start()
    per = steps * rows
    here = lax.axis_index("narrow")
    out, src = iotas(tokens)
    row = lax.rem(out, rows)
    step = lax.rem(lax.div(out, rows), steps)
    d = lax.rem(lax.div(out, per), wide)
    owner = lax.bitwise_xor(lax.div(out, per * wide), here)
    order = (src == ((d * steps + step) * narrow + owner) * rows + row).astype(BF16)
    squares = jnp.zeros((tokens, 1), F32)
    for at, size in chunks(depth, 512):
        x = jnp.concatenate([b[:, at : at + size] for b in blocks], axis=0)
        part = jnp.dot(order, x, preferred_element_type=F32)
        squares = squares + jnp.sum(part * part, axis=1, keepdims=True)
        scaled[:, at : at + size] = (part * gain_ref[:, at : at + size].astype(F32)).astype(BF16)
    high = squares.astype(BF16).astype(F32)
    lane = lax.broadcasted_iota(jnp.int32, (tokens, LANES), 1)
    head = jnp.where(lane == 0, high, jnp.where(lane == 1, squares - high, 0.0)).astype(BF16)
    span = per * wide
    for e in range(narrow):
        outs[e][:, :LANES] = head[e * span : (e + 1) * span]
    for at, size in chunks(width, 768):
        acc[:, at : at + size] = jnp.dot(
            scaled[:, :split], near_ref[:, at : at + size], preferred_element_type=F32
        )
    for i, (low, deep) in enumerate(chunks(depth - split, 512)):
        rest[i].wait()
        for at, size in chunks(width, 768):
            y = acc[:, at : at + size] + jnp.dot(
                scaled[:, split + low : split + low + deep],
                far[low : low + deep, at : at + size],
                preferred_element_type=F32,
            )
            if i < len(rest) - 1:
                acc[:, at : at + size] = y
                continue
            y = y.astype(BF16)
            for e in range(narrow):
                outs[e][:, LANES + at : LANES + at + size] = y[e * span : (e + 1) * span]


def normalize_kernel(wide, narrow, model, *refs):
    parts, outs = refs[:narrow], refs[-wide:]
    per = outs[0].shape[0]
    head = sum(p[:, :LANES].astype(F32) for p in parts)
    factor = lax.rsqrt((head[:, 0:1] + head[:, 1:2]) / model + norm_epsilon)
    total = sum(p[:, LANES:].astype(F32) for p in parts) * factor
    for d in range(wide):
        outs[d][...] = total[d * per : (d + 1) * per].astype(BF16)


def attend_kernel(wide, steps, slice_width, *refs):
    mask_ref, parts = refs[0], refs[1 : 1 + wide]
    cos_ref, sin_ref, key_ref, value_ref = refs[1 + wide : 5 + wide]
    outs, (stack, proj, query, total) = refs[-4 - wide : -4], refs[-4:]
    rows, kv_heads, slots, head_dim = key_ref.shape
    width = parts[0].shape[1]
    width_query = slice_width * wide
    heads = width_query // head_dim
    group = heads // kv_heads
    scale = head_dim ** (-0.5) * math.log2(math.e)
    here = lax.axis_index("wide")

    for d in range(wide):
        stack[d] = parts[d][...].astype(F32)
    for w in range(wide):
        proj[:, w * width : (w + 1) * width] = stack[lax.bitwise_xor(here, w)]

    cosine = cos_ref[...]
    sine = sin_ref[...]

    def turned(at):
        x = proj[:, at : at + head_dim]
        return (x * cosine + pltpu.roll(x, head_dim // 2, 1) * sine).astype(BF16).astype(F32)

    for h in range(heads):
        q = turned(h * head_dim)
        for s in range(steps):
            for r in range(rows):
                i = s * rows + r
                at = s * group + h % group
                query[h // group, r, at : at + 1, :] = q[i : i + 1]
    step_of = lax.div(lax.broadcasted_iota(jnp.int32, (steps * group, 1), 0), group)

    def compare(k):
        return [
            lax.dot_general(
                query[k, r].astype(BF16), key_ref[r, k], (((1,), (1,)), ((), ())), preferred_element_type=F32
            )
            for r in range(rows)
        ]

    def weigh(k, scores):
        fresh_key = turned(width_query + k * head_dim)
        made = []
        for r in range(rows):
            cached = scores[r] + mask_ref[r : r + 1]
            highest = jnp.max(cached, axis=1, keepdims=True)
            newest = []
            for j in range(steps):
                i = j * rows + r
                dot = jnp.sum(query[k, r] * fresh_key[i : i + 1], axis=1, keepdims=True)
                newest.append(jnp.where(step_of >= j, dot, -jnp.inf))
                highest = jnp.maximum(highest, newest[-1])
            weights = jnp.exp2((cached - highest) * scale)
            denominator = jnp.sum(weights, axis=1, keepdims=True)
            fresh = [jnp.exp2((dot - highest) * scale) for dot in newest]
            for weight in fresh:
                denominator = denominator + weight
            made.append((weights.astype(BF16), fresh, denominator))
        return made

    def combine(k, made):
        at = width_query + (kv_heads + k) * head_dim
        fresh_value = proj[:, at : at + head_dim]
        for r, (weights, fresh, denominator) in enumerate(made):
            out = jnp.dot(weights, value_ref[r, k], preferred_element_type=F32)
            for j, weight in enumerate(fresh):
                i = j * rows + r
                out = out + weight.astype(BF16).astype(F32) * fresh_value[i : i + 1]
            out = out / denominator
            for s in range(steps):
                for g in range(group):
                    at = (k * group + g) * head_dim
                    w, col = at // slice_width, at % slice_width
                    i = s * rows + r
                    total[w, i : i + 1, col : col + head_dim] = out[s * group + g : s * group + g + 1]

    scores, ready = compare(0), None
    for k in range(kv_heads):
        following = compare(k + 1) if k + 1 < kv_heads else None
        made = weigh(k, scores)
        if ready:
            combine(*ready)
        ready, scores = (k, made), following
    combine(*ready)
    for d in range(wide):
        outs[d][...] = total[lax.bitwise_xor(here, d)].astype(BF16)


def join_kernel(*refs):
    per = refs[0].shape[0]
    scratch = refs[-1]
    for d, ref in enumerate(refs[:-2]):
        scratch[d * per : (d + 1) * per] = ref[...].astype(F32)
    refs[-2][...] = scratch[...].astype(BF16)


def output_kernel(wide, narrow, steps, rows, *refs):
    blocks, (early_ref, late_ref, w_ref) = refs[:narrow], refs[narrow : narrow + 3]
    keep_ref, send_ref, ordered, acc, last, sem = refs[narrow + 3 :]
    ends = [early_ref.shape[0], early_ref.shape[0] + late_ref.shape[0], w_ref.shape[0]]
    rest = pltpu.make_async_copy(w_ref.at[pl.ds(ends[1], ends[2] - ends[1])], last, sem)
    rest.start()
    block, depth = blocks[0].shape
    tokens = block * narrow
    per = steps * rows
    here = lax.axis_index("narrow")
    out, src = iotas(tokens)
    row = lax.rem(out, rows)
    owner = lax.rem(lax.div(out, rows), narrow)
    step = lax.rem(lax.div(out, rows * narrow), steps)
    d = lax.div(out, per * narrow)
    d = lax.rem(d, wide // 2) * 2 + lax.div(d, wide // 2)
    e = lax.bitwise_xor(owner, here)
    order = (src == ((e * wide + d) * steps + step) * rows + row).astype(BF16)
    for at, size in chunks(depth, 512):
        x = jnp.concatenate([b[:, at : at + size] for b in blocks], axis=0)
        ordered[:, at : at + size] = jnp.dot(order, x, preferred_element_type=F32).astype(BF16)
    half = tokens // 2
    for i, (piece, begin, end) in enumerate(zip((early_ref, late_ref, last), [0] + ends, ends)):
        if i == 2:
            rest.wait()
        for at, size in chunks(w_ref.shape[1], 512):
            y = jnp.dot(ordered[:, begin:end], piece[:, at : at + size], preferred_element_type=F32)
            if i:
                y = y + acc[:, at : at + size]
            if i < 2:
                acc[:, at : at + size] = y
                continue
            keep_ref[:, at : at + size] = y[:half]
            send_ref[:, at : at + size] = y[half:].astype(BF16)


def pair_kernel(keep_ref, other_ref, *outs):
    block = outs[0].shape[0]
    for x, out in enumerate(outs):
        span = pl.ds(x * block, block)
        out[...] = (keep_ref[span] + other_ref[span].astype(F32)).astype(out.dtype)


def total_kernel(*refs):
    refs[-1][...] = sum(ref[...].astype(F32) for ref in refs[:-1]).astype(BF16)


def call(kernel, name, outs, inputs, scratch=(), specs=None, flops=0, size=0, exps=0):
    return pl.pallas_call(
        kernel,
        out_shape=outs,
        in_specs=specs or [whole()] * len(inputs),
        out_specs=jax.tree.map(lambda _: whole(), outs),
        scratch_shapes=list(scratch),
        compiler_params=params(),
        cost_estimate=pl.CostEstimate(flops=flops, bytes_accessed=size, transcendentals=exps),
        name=name,
    )(*inputs)


def body(hidden_in, norm_gain, qkv_weight, out_weight, lengths, key_cache, cache_of_values):
    wide = lax.axis_size("wide")
    narrow = lax.axis_size("narrow")
    steps, block_rows, depth = hidden_in.shape
    rows, kv_heads, slots, head_dim = key_cache.shape
    width = qkv_weight.shape[1]
    slice_width, out_width = out_weight.shape
    block = steps * block_rows
    tokens = block * wide
    per = steps * rows
    heads = slice_width * wide // head_dim
    shape = jax.ShapeDtypeStruct

    half = np.arange(head_dim) % (head_dim // 2)
    freqs = np.asarray(rope_base ** (-2.0 * half / head_dim), np.float32)[None]
    qkv_split = depth // 2
    early, late = slice_width // 4, slice_width // 2

    (qkv_near,) = fetch([(qkv_weight, 0, qkv_split)], [])
    with jax.named_scope("gather_tokens"):
        own = hidden_in.reshape(block, depth)
        blocks = []
        for x in range(wide // 2):
            near = swap(own, "wide", 2 * x) if x else own
            if x:
                near, qkv_near = lax.optimization_barrier((near, qkv_near))
            blocks += [near, swap(near, "wide", 1)]
    partial = call(
        functools.partial(project_kernel, wide, narrow, steps, rows), "project",
        [shape((per * wide, LANES + width), BF16)] * narrow,
        blocks
        + [norm_gain.reshape(1, -1), resident(qkv_near), pltpu.with_memory_space_constraint(qkv_weight, pltpu.HBM)],
        [
            pltpu.VMEM((tokens, depth), BF16),
            pltpu.VMEM((tokens, width), F32),
            pltpu.VMEM((depth - qkv_split, width), BF16),
            pltpu.SemaphoreType.DMA((-(-(depth - qkv_split) // 512),)),
        ],
        [whole()] * (wide + 2) + [pl.BlockSpec(memory_space=pltpu.HBM)],
        flops=2 * tokens * depth * width, size=2 * depth * width,
    )
    keys, values, cosine, sine, mask = fetch(
        [(key_cache, 0, rows), (cache_of_values, 0, rows)],
        [partial[0]],
        (steps, lengths, jnp.asarray(freqs)),
    )
    with jax.named_scope("sum_over_narrow"):
        parts = [swap(partial[e], "narrow", e) if e else partial[e] for e in reversed(range(narrow))]
    normed = call(
        functools.partial(normalize_kernel, wide, narrow, depth * narrow), "normalize",
        [shape((per, width), BF16)] * wide,
        parts + [cosine],
        specs=[whole()] * narrow + [hbm()],
        size=4 * tokens * width,
    )
    (out_early,) = fetch([(out_weight, 0, early)], [normed[0]])
    with jax.named_scope("columns_to_owner"):
        mine = [swap(p, "wide", d) if d else p for d, p in enumerate(normed)]
    attended = call(
        functools.partial(attend_kernel, wide, steps, slice_width), "attend",
        [shape((per, slice_width), BF16)] * wide,
        [mask] + mine + [cosine, sine, resident(keys), resident(values), out_early],
        [
            pltpu.VMEM((wide, per, width), F32),
            pltpu.VMEM((per, width * wide), F32),
            pltpu.VMEM((kv_heads, rows, steps * heads // kv_heads, head_dim), F32),
            pltpu.VMEM((wide, per, slice_width), F32),
        ],
        [whole()] * (wide + 5) + [hbm()],
        flops=4 * per * heads * slots * head_dim,
        size=4 * rows * kv_heads * slots * head_dim,
        exps=per * heads * slots,
    )
    with jax.named_scope("heads_to_weights"):
        arrived = [swap(p, "wide", d) if d else p for d, p in enumerate(attended)]
    joined = call(
        join_kernel, "join", shape((per * wide, slice_width), BF16), arrived,
        [pltpu.VMEM((per * wide, slice_width), F32)], size=4 * per * wide * slice_width,
    )
    (out_late,) = fetch([(out_weight, early, late)], [joined])
    with jax.named_scope("gather_over_narrow"):
        spread = [swap(joined, "narrow", e) if e else joined for e in range(narrow)]
    keep, send = call(
        functools.partial(output_kernel, wide, narrow, steps, rows), "output",
        [shape((tokens // 2, out_width), F32), shape((tokens // 2, out_width), BF16)],
        spread
        + [resident(out_early), resident(out_late), pltpu.with_memory_space_constraint(out_weight, pltpu.HBM)],
        [
            pltpu.VMEM((tokens, slice_width), BF16),
            pltpu.VMEM((tokens, out_width), F32),
            pltpu.VMEM((slice_width - early - late, out_width), BF16),
            pltpu.SemaphoreType.DMA,
        ],
        [whole()] * (narrow + 2) + [pl.BlockSpec(memory_space=pltpu.HBM)],
        flops=2 * tokens * slice_width * out_width, size=2 * slice_width * out_width,
    )
    with jax.named_scope("sum_over_wide"):
        other = swap(send, "wide", 1)
        chip = call(
            pair_kernel, "pair",
            [shape((block, out_width), BF16 if x else F32) for x in range(wide // 2)],
            [keep, other], size=6 * tokens * out_width // 2,
        )
        sums = [swap(c, "wide", 2 * x) if x else c for x, c in enumerate(chip)]
    total = call(
        total_kernel, "total", shape((block, out_width), BF16), sums, size=8 * block * out_width
    )
    return total.reshape(steps, block_rows, out_width)


def solution(mesh):
    in_specs = (
        P(None, ("groups", "wide"), "narrow"),
        P("narrow"),
        P("narrow", "wide"),
        P("wide", "narrow"),
        P(("groups", "wide", "narrow")),
        P(("groups", "wide", "narrow"), None, None, None),
        P(("groups", "wide", "narrow"), None, None, None),
    )
    out_specs = P(None, ("groups", "wide"), "narrow")
    return jax.shard_map(body, mesh=mesh, in_specs=in_specs, out_specs=out_specs, check_vma=False)
```

```python
import functools
import math

import jax
import jax.numpy as jnp
import numpy as np
from jax import lax
from jax.experimental import pallas as pl
from jax.experimental.pallas import tpu as pltpu
from jax.sharding import PartitionSpec as P

F32 = jnp.float32
BF16 = jnp.bfloat16
LANES = 128
MIB = 1 << 20
norm_epsilon = 1e-05
rope_base = 500000.0


def chunks(total, size):
    return [(at, min(size, total - at)) for at in range(0, total, size)]


def iotas(tokens):
    out = lax.broadcasted_iota(jnp.int32, (tokens, tokens), 0)
    src = lax.broadcasted_iota(jnp.int32, (tokens, tokens), 1)
    return out, src


def whole():
    return pl.BlockSpec(memory_space=pltpu.VMEM)


def hbm():
    return pl.BlockSpec(memory_space=pl.ANY)


def params():
    return pltpu.CompilerParams(vmem_limit_bytes=16 * MIB)


def swap(array, axis, distance):
    size = lax.axis_size(axis)
    return lax.ppermute(array, axis, [(i, i ^ distance) for i in range(size)])


def resident(array):
    return pltpu.with_memory_space_constraint(array, pltpu.VMEM)


def fetch_kernel(spans, turns, *refs):
    count = len(spans)
    sources, sem = refs[:count], refs[-1]
    outs = refs[len(refs) - 1 - count - 3 * bool(turns) : -1]
    copies = []
    for i, (at, size) in enumerate(spans):
        copies.append(pltpu.make_async_copy(sources[i].at[pl.ds(at, size)], outs[i], sem.at[i]))
    for copy in copies:
        copy.start()
    if turns:
        steps, rows = turns
        lengths_ref, freqs_ref = refs[count : count + 2]
        cos_ref, sin_ref, mask_ref = outs[-3:]
        for s in range(steps):
            for r in range(rows):
                i = s * rows + r
                angle = (lengths_ref[r] + s).astype(F32) * freqs_ref[...]
                lane = lax.broadcasted_iota(jnp.int32, angle.shape, 1)
                cos_ref[i : i + 1] = jnp.cos(angle)
                sin_ref[i : i + 1] = jnp.where(lane < angle.shape[1] // 2, -1.0, 1.0) * jnp.sin(angle)
        slot = lax.broadcasted_iota(jnp.int32, (1, mask_ref.shape[1]), 1)
        for r in range(rows):
            mask_ref[r : r + 1] = jnp.where(slot < lengths_ref[r], 0.0, -jnp.inf)
    for copy in copies:
        copy.wait()


def fetch(spans, after, turns=()):
    arrays = [pltpu.with_memory_space_constraint(a, pltpu.HBM) for a, _, _ in spans]
    outs = [pltpu.VMEM((n,) + a.shape[1:], a.dtype) for a, _, n in spans]
    size = sum(2 * n * a.size // a.shape[0] * a.dtype.itemsize for a, _, n in spans)
    extra, extra_specs = [], []
    if turns:
        steps, lengths, freqs = turns
        turns = (steps, lengths.shape[0])
        extra, extra_specs = [lengths, freqs], [pl.BlockSpec(memory_space=pltpu.SMEM), whole()]
        outs += [jax.ShapeDtypeStruct((steps * lengths.shape[0], freqs.shape[1]), F32)] * 2
        outs += [jax.ShapeDtypeStruct((lengths.shape[0], arrays[0].shape[2]), F32)]
    return pl.pallas_call(
        functools.partial(fetch_kernel, [(at, n) for _, at, n in spans], turns),
        out_shape=outs,
        in_specs=[pl.BlockSpec(memory_space=pltpu.HBM)] * len(arrays) + extra_specs + [hbm()] * len(after),
        out_specs=[whole()] * len(outs),
        scratch_shapes=[pltpu.SemaphoreType.DMA((len(arrays),))],
        compiler_params=params(),
        cost_estimate=pl.CostEstimate(flops=0, bytes_accessed=size, transcendentals=0),
        name="fetch",
    )(*arrays, *extra, *after)


def project_kernel(wide, narrow, steps, rows, *refs):
    blocks, (gain_ref, near_ref, w_ref) = refs[:wide], refs[wide : wide + 3]
    outs, (scaled, acc, far, sem) = refs[wide + 3 : -4], refs[-4:]
    block, depth = blocks[0].shape
    tokens = block * wide
    split, width = near_ref.shape
    rest = []
    for i, (at, size) in enumerate(chunks(depth - split, 512)):
        rest.append(
            pltpu.make_async_copy(w_ref.at[pl.ds(split + at, size)], far.at[pl.ds(at, size)], sem.at[i])
        )
        rest[-1].start()
    per = steps * rows
    here = lax.axis_index("narrow")
    out, src = iotas(tokens)
    row = lax.rem(out, rows)
    step = lax.rem(lax.div(out, rows), steps)
    d = lax.rem(lax.div(out, per), wide)
    owner = lax.bitwise_xor(lax.div(out, per * wide), here)
    order = (src == ((d * steps + step) * narrow + owner) * rows + row).astype(BF16)
    squares = jnp.zeros((tokens, 1), F32)
    for at, size in chunks(depth, 512):
        x = jnp.concatenate([b[:, at : at + size] for b in blocks], axis=0)
        part = jnp.dot(order, x, preferred_element_type=F32)
        squares = squares + jnp.sum(part * part, axis=1, keepdims=True)
        scaled[:, at : at + size] = (part * gain_ref[:, at : at + size].astype(F32)).astype(BF16)
    high = squares.astype(BF16).astype(F32)
    lane = lax.broadcasted_iota(jnp.int32, (tokens, LANES), 1)
    head = jnp.where(lane == 0, high, jnp.where(lane == 1, squares - high, 0.0)).astype(BF16)
    span = per * wide
    for e in range(narrow):
        outs[e][:, :LANES] = head[e * span : (e + 1) * span]
    for at, size in chunks(width, 768):
        acc[:, at : at + size] = jnp.dot(
            scaled[:, :split], near_ref[:, at : at + size], preferred_element_type=F32
        )
    for i, (low, deep) in enumerate(chunks(depth - split, 512)):
        rest[i].wait()
        for at, size in chunks(width, 768):
            y = acc[:, at : at + size] + jnp.dot(
                scaled[:, split + low : split + low + deep],
                far[low : low + deep, at : at + size],
                preferred_element_type=F32,
            )
            if i < len(rest) - 1:
                acc[:, at : at + size] = y
                continue
            y = y.astype(BF16)
            for e in range(narrow):
                outs[e][:, LANES + at : LANES + at + size] = y[e * span : (e + 1) * span]


def normalize_kernel(wide, narrow, model, *refs):
    parts, outs = refs[:narrow], refs[-wide:]
    per = outs[0].shape[0]
    head = sum(p[:, :LANES].astype(F32) for p in parts)
    factor = lax.rsqrt((head[:, 0:1] + head[:, 1:2]) / model + norm_epsilon)
    total = sum(p[:, LANES:].astype(F32) for p in parts) * factor
    for d in range(wide):
        outs[d][...] = total[d * per : (d + 1) * per].astype(BF16)


def assemble(parts, proj, stack):
    wide, width = len(parts), parts[0].shape[1]
    here = lax.axis_index("wide")
    for d in range(wide):
        stack[d] = parts[d][...].astype(F32)
    for w in range(wide):
        proj[:, w * width : (w + 1) * width] = stack[lax.bitwise_xor(here, w)]


def attend_kernel(wide, steps, slice_width, far, *refs):
    count = wide if far else 1
    parts, (mask_ref, cos_ref, sin_ref, key_ref, value_ref) = refs[:count], refs[count : count + 5]
    near = wide // 2
    if far:
        outs, (proj, stack, query, total) = refs[-4 - near : -4], refs[-4:]
        assemble(parts, proj, stack)
    else:
        outs, proj, (query, total) = refs[-2 - near : -2], parts[0], refs[-2:]
    rows, kv_heads, slots, head_dim = key_ref.shape
    width_query = slice_width * wide
    heads = width_query // head_dim
    group = heads // kv_heads
    scale = head_dim ** (-0.5) * math.log2(math.e)
    here = lax.axis_index("wide")
    half = lax.div(here, near)
    half = 1 - half if far else half
    first = half * (kv_heads // 2)

    cosine = cos_ref[...]
    sine = sin_ref[...]

    def columns(at):
        return proj[:, pl.ds(pl.multiple_of(at, LANES), head_dim)]

    def turned(at):
        x = columns(at)
        return (x * cosine + pltpu.roll(x, head_dim // 2, 1) * sine).astype(BF16).astype(F32)

    for h in range(heads // 2):
        q = turned((first * group + h) * head_dim)
        for s in range(steps):
            for r in range(rows):
                i = s * rows + r
                at = s * group + h % group
                query[h // group, r, at : at + 1, :] = q[i : i + 1]
    step_of = lax.div(lax.broadcasted_iota(jnp.int32, (steps * group, 1), 0), group)

    def compare(k):
        return [
            lax.dot_general(
                query[k, r].astype(BF16),
                key_ref[r, first + k],
                (((1,), (1,)), ((), ())),
                preferred_element_type=F32,
            )
            for r in range(rows)
        ]

    def weigh(k, scores):
        fresh_key = turned(width_query + (first + k) * head_dim)
        made = []
        for r in range(rows):
            cached = scores[r] + mask_ref[r : r + 1]
            highest = jnp.max(cached, axis=1, keepdims=True)
            newest = []
            for j in range(steps):
                i = j * rows + r
                dot = jnp.sum(query[k, r] * fresh_key[i : i + 1], axis=1, keepdims=True)
                newest.append(jnp.where(step_of >= j, dot, -jnp.inf))
                highest = jnp.maximum(highest, newest[-1])
            weights = jnp.exp2((cached - highest) * scale)
            denominator = jnp.sum(weights, axis=1, keepdims=True)
            fresh = [jnp.exp2((dot - highest) * scale) for dot in newest]
            for weight in fresh:
                denominator = denominator + weight
            made.append((weights.astype(BF16), fresh, denominator))
        return made

    def combine(k, made):
        fresh_value = columns(width_query + (kv_heads + first + k) * head_dim)
        for r, (weights, fresh, denominator) in enumerate(made):
            out = jnp.dot(weights, value_ref[r, first + k], preferred_element_type=F32)
            for j, weight in enumerate(fresh):
                i = j * rows + r
                out = out + weight.astype(BF16).astype(F32) * fresh_value[i : i + 1]
            out = out / denominator
            for s in range(steps):
                for g in range(group):
                    at = (k * group + g) * head_dim
                    w, col = at // slice_width, at % slice_width
                    i = s * rows + r
                    total[w, i : i + 1, col : col + head_dim] = out[s * group + g : s * group + g + 1]

    scores, ready = compare(0), None
    for k in range(kv_heads // 2):
        following = compare(k + 1) if k + 1 < kv_heads // 2 else None
        made = weigh(k, scores)
        if ready:
            combine(*ready)
        ready, scores = (k, made), following
    combine(*ready)
    for d in range(near):
        outs[d][...] = total[lax.bitwise_xor(lax.rem(here, near), d)].astype(BF16)


def join_kernel(order, *refs):
    per = refs[0].shape[0]
    scratch = refs[-1]
    for d, ref in zip(order, refs):
        scratch[d * per : (d + 1) * per] = ref[...].astype(F32)
    refs[-2][...] = scratch[...].astype(BF16)


def arrange_kernel(wide, narrow, steps, rows, *refs):
    blocks, ordered = refs[:narrow], refs[-1]
    block, depth = blocks[0].shape
    tokens = block * narrow
    per = steps * rows
    here = lax.axis_index("narrow")
    out, src = iotas(tokens)
    row = lax.rem(out, rows)
    owner = lax.rem(lax.div(out, rows), narrow)
    step = lax.rem(lax.div(out, rows * narrow), steps)
    d = lax.div(out, per * narrow)
    d = lax.rem(d, wide // 2) * 2 + lax.div(d, wide // 2)
    place = narrow - 1 - lax.bitwise_xor(owner, here)
    order = (src == ((place * wide + d) * steps + step) * rows + row).astype(BF16)
    for at, size in chunks(depth, 512):
        x = jnp.concatenate([b[:, at : at + size] for b in blocks], axis=0)
        ordered[:, at : at + size] = jnp.dot(order, x, preferred_element_type=F32).astype(BF16)


def output_kernel(first, arrange, *refs):
    inputs, (keep_ref, send_ref) = refs[: -2 - bool(arrange)], refs[-2:]
    blocks, pieces = inputs[:-3], inputs[-3:]
    half, span = keep_ref.shape
    if arrange:
        ordered = refs[-3]
        arrange(*blocks, ordered)
    else:
        ordered = blocks[0]
    for at, size in chunks(span, 512):
        y, begin = 0.0, 0
        for piece in pieces:
            end = begin + piece.shape[0]
            y = y + jnp.dot(
                ordered[:, begin:end], piece[:, first + at : first + at + size], preferred_element_type=F32
            )
            begin = end
        keep_ref[:, at : at + size] = y[:half]
        send_ref[:, at : at + size] = y[half:].astype(BF16)


def pair_kernel(keep_ref, other_ref, *outs):
    block = outs[0].shape[0]
    for x, out in enumerate(outs):
        span = pl.ds(x * block, block)
        out[...] = (keep_ref[span] + other_ref[span].astype(F32)).astype(out.dtype)


def total_kernel(*refs):
    count = refs[-1].shape[1] // refs[0].shape[1]
    each = (len(refs) - 1) // count
    span = refs[0].shape[1]
    for i in range(count):
        part = refs[i * each : (i + 1) * each]
        refs[-1][:, i * span : (i + 1) * span] = sum(ref[...].astype(F32) for ref in part).astype(BF16)


def call(kernel, name, outs, inputs, scratch=(), specs=None, flops=0, size=0, exps=0):
    return pl.pallas_call(
        kernel,
        out_shape=outs,
        in_specs=specs or [whole()] * len(inputs),
        out_specs=jax.tree.map(lambda _: whole(), outs),
        scratch_shapes=list(scratch),
        compiler_params=params(),
        cost_estimate=pl.CostEstimate(flops=flops, bytes_accessed=size, transcendentals=exps),
        name=name,
    )(*inputs)


def body(hidden_in, norm_gain, qkv_weight, out_weight, lengths, key_cache, cache_of_values):
    wide = lax.axis_size("wide")
    narrow = lax.axis_size("narrow")
    steps, block_rows, depth = hidden_in.shape
    rows, kv_heads, slots, head_dim = key_cache.shape
    width = qkv_weight.shape[1]
    slice_width, out_width = out_weight.shape
    block = steps * block_rows
    tokens = block * wide
    per = steps * rows
    heads = slice_width * wide // head_dim
    shape = jax.ShapeDtypeStruct

    half = np.arange(head_dim) % (head_dim // 2)
    freqs = np.asarray(rope_base ** (-2.0 * half / head_dim), np.float32)[None]
    qkv_split = depth // 2
    quarter = slice_width // 4

    (qkv_near,) = fetch([(qkv_weight, 0, qkv_split)], [])
    with jax.named_scope("gather_tokens"):
        own = hidden_in.reshape(block, depth)
        blocks = []
        for x in range(wide // 2):
            near = swap(own, "wide", 2 * x) if x else own
            if x:
                near, qkv_near = lax.optimization_barrier((near, qkv_near))
            blocks += [near, swap(near, "wide", 1)]
    partial = call(
        functools.partial(project_kernel, wide, narrow, steps, rows), "project",
        [shape((per * wide, LANES + width), BF16)] * narrow,
        blocks
        + [norm_gain.reshape(1, -1), resident(qkv_near), pltpu.with_memory_space_constraint(qkv_weight, pltpu.HBM)],
        [
            pltpu.VMEM((tokens, depth), BF16),
            pltpu.VMEM((tokens, width), F32),
            pltpu.VMEM((depth - qkv_split, width), BF16),
            pltpu.SemaphoreType.DMA((-(-(depth - qkv_split) // 512),)),
        ],
        [whole()] * (wide + 2) + [pl.BlockSpec(memory_space=pltpu.HBM)],
        flops=2 * tokens * depth * width, size=2 * depth * width,
    )
    keys, values, out_first, cosine, sine, mask = fetch(
        [(key_cache, 0, rows), (cache_of_values, 0, rows), (out_weight, 0, quarter)],
        [partial[0]],
        (steps, lengths, jnp.asarray(freqs)),
    )
    with jax.named_scope("sum_over_narrow"):
        parts = [swap(partial[e], "narrow", e) if e else partial[e] for e in reversed(range(narrow))]
    normed = call(
        functools.partial(normalize_kernel, wide, narrow, depth * narrow), "normalize",
        [shape((per, width), BF16)] * wide,
        parts + [cosine],
        specs=[whole()] * narrow + [hbm()],
        size=4 * tokens * width,
    )
    (out_second,) = fetch([(out_weight, quarter, quarter)], [normed[0]])
    with jax.named_scope("columns_to_owner"):
        mine = [swap(p, "wide", d) if d else p for d, p in enumerate(normed)]
    common = [mask, cosine, sine, resident(keys), resident(values)]
    scratch = [
        pltpu.VMEM((kv_heads // 2, rows, steps * heads // kv_heads, head_dim), F32),
        pltpu.VMEM((wide // 2, per, slice_width), F32),
    ]
    arrived, inputs, extra = {}, mine, [out_second]
    for far in (True, False):
        results = call(
            functools.partial(attend_kernel, wide, steps, slice_width, far), "attend",
            [shape((per, slice_width), BF16)] * (wide // 2) + ([shape((per, width * wide), F32)] if far else []),
            inputs + common + extra,
            ([pltpu.VMEM((wide, per, width), F32)] if far else []) + scratch,
            [whole()] * (len(inputs) + 5) + [hbm()] * len(extra),
            flops=2 * per * heads * slots * head_dim,
            size=2 * rows * kv_heads * slots * head_dim,
            exps=per * heads * slots // 2,
        )
        with jax.named_scope("heads_to_weights"):
            outs = results[: wide // 2]
            if not far:
                outs, arrived = lax.optimization_barrier((outs, arrived))
            for i in range(wide // 2):
                d = i + wide // 2 * far
                arrived[d] = swap(outs[i], "wide", d) if d else outs[i]
        inputs, extra = [results[-1]], []
    joined = call(
        functools.partial(join_kernel, list(arrived)), "join", shape((per * wide, slice_width), BF16),
        list(arrived.values()),
        [pltpu.VMEM((per * wide, slice_width), F32)], size=4 * per * wide * slice_width,
    )
    (out_last,) = fetch([(out_weight, 2 * quarter, 2 * quarter)], [joined])
    with jax.named_scope("gather_over_narrow"):
        spread = [swap(joined, "narrow", e) if e else joined for e in reversed(range(narrow))]
    weights = [resident(out_first), resident(out_second), resident(out_last)]
    span = out_width // 2
    made = [shape((tokens // 2, span), F32), shape((tokens // 2, span), BF16)]
    arrange = functools.partial(arrange_kernel, wide, narrow, steps, rows)
    inputs, sums = spread, []
    for i in range(2):
        results = call(
            functools.partial(output_kernel, i * span, None if i else arrange), "output",
            ([] if i else [shape((tokens, slice_width), BF16)]) + made,
            inputs + weights,
            flops=2 * tokens * slice_width * span, size=2 * slice_width * span,
        )
        if not i:
            inputs, results = list(results[:1]), results[1:]
        keep, send = results
        with jax.named_scope("sum_over_wide"):
            other = swap(send, "wide", 1)
            chip = call(
                pair_kernel, "pair",
                [shape((block, span), BF16 if x else F32) for x in range(wide // 2)],
                [keep, other], size=6 * tokens * span // 2,
            )
            sums += [swap(c, "wide", 2 * x) if x else c for x, c in enumerate(chip)]
    total = call(
        total_kernel, "total", shape((block, out_width), BF16), sums, size=8 * block * out_width
    )
    return total.reshape(steps, block_rows, out_width)


def solution(mesh):
    in_specs = (
        P(None, ("groups", "wide"), "narrow"),
        P("narrow"),
        P("narrow", "wide"),
        P("wide", "narrow"),
        P(("groups", "wide", "narrow")),
        P(("groups", "wide", "narrow"), None, None, None),
        P(("groups", "wide", "narrow"), None, None, None),
    )
    out_specs = P(None, ("groups", "wide"), "narrow")
    return jax.shard_map(body, mesh=mesh, in_specs=in_specs, out_specs=out_specs, check_vma=False)
```

```python
import functools
import math

import jax
import jax.numpy as jnp
import numpy as np
from jax import lax
from jax.experimental import pallas as pl
from jax.experimental.pallas import tpu as pltpu
from jax.sharding import PartitionSpec as P

F32 = jnp.float32
BF16 = jnp.bfloat16
LANES = 128
MIB = 1 << 20
norm_epsilon = 1e-05
rope_base = 500000.0


def chunks(total, size):
    return [(at, min(size, total - at)) for at in range(0, total, size)]


def iotas(tokens):
    out = lax.broadcasted_iota(jnp.int32, (tokens, tokens), 0)
    src = lax.broadcasted_iota(jnp.int32, (tokens, tokens), 1)
    return out, src


def whole():
    return pl.BlockSpec(memory_space=pltpu.VMEM)


def hbm():
    return pl.BlockSpec(memory_space=pl.ANY)


def params():
    return pltpu.CompilerParams(vmem_limit_bytes=16 * MIB)


def swap(array, axis, distance):
    size = lax.axis_size(axis)
    return lax.ppermute(array, axis, [(i, i ^ distance) for i in range(size)])


def resident(array):
    return pltpu.with_memory_space_constraint(array, pltpu.VMEM)


def fetch_kernel(spans, turns, *refs):
    count = len(spans)
    sources, sem = refs[:count], refs[-1]
    outs = refs[len(refs) - 1 - count - 3 * bool(turns) : -1]
    copies = []
    for i, (at, size) in enumerate(spans):
        copies.append(pltpu.make_async_copy(sources[i].at[pl.ds(at, size)], outs[i], sem.at[i]))
    for copy in copies:
        copy.start()
    if turns:
        steps, rows = turns
        lengths_ref, freqs_ref = refs[count : count + 2]
        cos_ref, sin_ref, mask_ref = outs[-3:]
        for s in range(steps):
            for r in range(rows):
                i = s * rows + r
                angle = (lengths_ref[:, r : r + 1] + s).astype(F32) * freqs_ref[...]
                lane = lax.broadcasted_iota(jnp.int32, angle.shape, 1)
                cos_ref[i : i + 1] = jnp.cos(angle)
                sin_ref[i : i + 1] = jnp.where(lane < angle.shape[1] // 2, -1.0, 1.0) * jnp.sin(angle)
        slot = lax.broadcasted_iota(jnp.int32, (1, mask_ref.shape[1]), 1)
        for r in range(rows):
            mask_ref[r : r + 1] = jnp.where(slot < lengths_ref[:, r : r + 1], 0.0, -jnp.inf)
    for copy in copies:
        copy.wait()


def fetch(spans, after, turns=()):
    arrays = [pltpu.with_memory_space_constraint(a, pltpu.HBM) for a, _, _ in spans]
    outs = [pltpu.VMEM((n,) + a.shape[1:], a.dtype) for a, _, n in spans]
    size = sum(2 * n * a.size // a.shape[0] * a.dtype.itemsize for a, _, n in spans)
    extra, extra_specs = [], []
    if turns:
        steps, lengths, freqs = turns
        turns = (steps, lengths.shape[0])
        extra, extra_specs = [lengths.reshape(1, -1), freqs], [whole()] * 2
        outs += [jax.ShapeDtypeStruct((steps * lengths.shape[0], freqs.shape[1]), F32)] * 2
        outs += [jax.ShapeDtypeStruct((lengths.shape[0], arrays[0].shape[2]), F32)]
    return pl.pallas_call(
        functools.partial(fetch_kernel, [(at, n) for _, at, n in spans], turns),
        out_shape=outs,
        in_specs=[pl.BlockSpec(memory_space=pltpu.HBM)] * len(arrays) + extra_specs + [hbm()] * len(after),
        out_specs=[whole()] * len(outs),
        scratch_shapes=[pltpu.SemaphoreType.DMA((len(arrays),))],
        compiler_params=params(),
        cost_estimate=pl.CostEstimate(flops=0, bytes_accessed=size, transcendentals=0),
        name="fetch",
    )(*arrays, *extra, *after)


def project_kernel(wide, narrow, steps, rows, *refs):
    blocks, (gain_ref, near_ref, w_ref) = refs[:wide], refs[wide : wide + 3]
    outs, (scaled, acc, far, sem) = refs[wide + 3 : -4], refs[-4:]
    block, depth = blocks[0].shape
    tokens = block * wide
    split, width = near_ref.shape
    rest = []
    for i, (at, size) in enumerate(chunks(depth - split, 512)):
        rest.append(
            pltpu.make_async_copy(w_ref.at[pl.ds(split + at, size)], far.at[pl.ds(at, size)], sem.at[i])
        )
        rest[-1].start()
    per = steps * rows
    here = lax.axis_index("narrow")
    out, src = iotas(tokens)
    row = lax.rem(out, rows)
    step = lax.rem(lax.div(out, rows), steps)
    d = lax.rem(lax.div(out, per), wide)
    owner = lax.bitwise_xor(lax.div(out, per * wide), here)
    order = (src == ((d * steps + step) * narrow + owner) * rows + row).astype(BF16)
    squares = jnp.zeros((tokens, 1), F32)
    for at, size in chunks(depth, 512):
        x = jnp.concatenate([b[:, at : at + size] for b in blocks], axis=0)
        part = jnp.dot(order, x, preferred_element_type=F32)
        squares = squares + jnp.sum(part * part, axis=1, keepdims=True)
        scaled[:, at : at + size] = (part * gain_ref[:, at : at + size].astype(F32)).astype(BF16)
    high = squares.astype(BF16).astype(F32)
    lane = lax.broadcasted_iota(jnp.int32, (tokens, LANES), 1)
    head = jnp.where(lane == 0, high, jnp.where(lane == 1, squares - high, 0.0)).astype(BF16)
    span = per * wide
    for e in range(narrow):
        outs[e][:, :LANES] = head[e * span : (e + 1) * span]
    for at, size in chunks(width, 768):
        acc[:, at : at + size] = jnp.dot(
            scaled[:, :split], near_ref[:, at : at + size], preferred_element_type=F32
        )
    for i, (low, deep) in enumerate(chunks(depth - split, 512)):
        rest[i].wait()
        for at, size in chunks(width, 768):
            y = acc[:, at : at + size] + jnp.dot(
                scaled[:, split + low : split + low + deep],
                far[low : low + deep, at : at + size],
                preferred_element_type=F32,
            )
            if i < len(rest) - 1:
                acc[:, at : at + size] = y
                continue
            y = y.astype(BF16)
            for e in range(narrow):
                outs[e][:, LANES + at : LANES + at + size] = y[e * span : (e + 1) * span]


def normalize_kernel(wide, narrow, model, *refs):
    parts, outs = refs[:narrow], refs[-wide:]
    per = outs[0].shape[0]
    head = sum(p[:, :LANES].astype(F32) for p in parts)
    factor = lax.rsqrt((head[:, 0:1] + head[:, 1:2]) / model + norm_epsilon)
    total = sum(p[:, LANES:].astype(F32) for p in parts) * factor
    for d in range(wide):
        outs[d][...] = total[d * per : (d + 1) * per].astype(BF16)


def assemble(parts, proj, stack):
    wide, width = len(parts), parts[0].shape[1]
    here = lax.axis_index("wide")
    for d in range(wide):
        stack[d] = parts[d][...].astype(F32)
    for w in range(wide):
        proj[:, w * width : (w + 1) * width] = stack[lax.bitwise_xor(here, w)]


def attend_kernel(wide, steps, slice_width, low, span, *refs):
    far = 2 * low == wide
    count = wide if far else 1
    parts, (mask_ref, cos_ref, sin_ref, key_ref, value_ref) = refs[:count], refs[count : count + 5]
    if far:
        outs, (proj, stack, query, total) = refs[-4 - span : -4], refs[-4:]
        assemble(parts, proj, stack)
    else:
        outs, proj, (query, total) = refs[-2 - span : -2], parts[0], refs[-2:]
    rows, kv_heads, slots, head_dim = key_ref.shape
    width_query = slice_width * wide
    heads = width_query // head_dim
    group = heads // kv_heads
    scale = head_dim ** (-0.5) * math.log2(math.e)
    here = lax.axis_index("wide")
    taken = kv_heads * span // wide
    first = lax.div(lax.bitwise_xor(here, low), span) * taken

    cosine = cos_ref[...]
    sine = sin_ref[...]

    def columns(at):
        return proj[:, pl.ds(pl.multiple_of(at, LANES), head_dim)]

    def turned(at):
        x = columns(at)
        return (x * cosine + pltpu.roll(x, head_dim // 2, 1) * sine).astype(BF16).astype(F32)

    for h in range(taken * group):
        q = turned((first * group + h) * head_dim)
        for s in range(steps):
            for r in range(rows):
                i = s * rows + r
                at = s * group + h % group
                query[h // group, r, at : at + 1, :] = q[i : i + 1]
    step_of = lax.div(lax.broadcasted_iota(jnp.int32, (steps * group, 1), 0), group)

    def compare(k):
        return [
            lax.dot_general(
                query[k, r].astype(BF16),
                key_ref[r, first + k],
                (((1,), (1,)), ((), ())),
                preferred_element_type=F32,
            )
            for r in range(rows)
        ]

    def weigh(k, scores):
        fresh_key = turned(width_query + (first + k) * head_dim)
        made = []
        for r in range(rows):
            cached = scores[r] + mask_ref[r : r + 1]
            highest = jnp.max(cached, axis=1, keepdims=True)
            newest = []
            for j in range(steps):
                i = j * rows + r
                dot = jnp.sum(query[k, r] * fresh_key[i : i + 1], axis=1, keepdims=True)
                newest.append(jnp.where(step_of >= j, dot, -jnp.inf))
                highest = jnp.maximum(highest, newest[-1])
            weights = jnp.exp2((cached - highest) * scale)
            denominator = jnp.sum(weights, axis=1, keepdims=True)
            fresh = [jnp.exp2((dot - highest) * scale) for dot in newest]
            for weight in fresh:
                denominator = denominator + weight
            made.append((weights.astype(BF16), fresh, denominator))
        return made

    def combine(k, made):
        fresh_value = columns(width_query + (kv_heads + first + k) * head_dim)
        for r, (weights, fresh, denominator) in enumerate(made):
            out = jnp.dot(weights, value_ref[r, first + k], preferred_element_type=F32)
            for j, weight in enumerate(fresh):
                i = j * rows + r
                out = out + weight.astype(BF16).astype(F32) * fresh_value[i : i + 1]
            out = out / denominator
            for s in range(steps):
                for g in range(group):
                    at = (k * group + g) * head_dim
                    w, col = at // slice_width, at % slice_width
                    i = s * rows + r
                    total[w, i : i + 1, col : col + head_dim] = out[s * group + g : s * group + g + 1]

    scores, ready = compare(0), None
    for k in range(taken):
        following = compare(k + 1) if k + 1 < taken else None
        made = weigh(k, scores)
        if ready:
            combine(*ready)
        ready, scores = (k, made), following
    combine(*ready)
    for d in range(span):
        outs[d][:, :slice_width] = total[lax.rem(lax.bitwise_xor(here, low + d), span)].astype(BF16)
        if far:
            outs[d][:, slice_width:] = jnp.zeros((steps * rows, LANES), BF16)


def join_kernel(order, *refs):
    per = refs[0].shape[0]
    scratch = refs[-1]
    for d, ref in zip(order, refs):
        scratch[d * per : (d + 1) * per] = ref[:, : scratch.shape[1]].astype(F32)
    refs[-2][...] = scratch[...].astype(BF16)


def arrange_kernel(wide, narrow, steps, rows, *refs):
    blocks, ordered = refs[:narrow], refs[-1]
    block, depth = blocks[0].shape
    tokens = block * narrow
    per = steps * rows
    here = lax.axis_index("narrow")
    out, src = iotas(tokens)
    row = lax.rem(out, rows)
    owner = lax.rem(lax.div(out, rows), narrow)
    step = lax.rem(lax.div(out, rows * narrow), steps)
    d = lax.div(out, per * narrow)
    d = lax.rem(d, wide // 2) * 2 + lax.div(d, wide // 2)
    place = narrow - 1 - lax.bitwise_xor(owner, here)
    order = (src == ((place * wide + d) * steps + step) * rows + row).astype(BF16)
    for at, size in chunks(depth, 512):
        x = jnp.concatenate([b[:, at : at + size] for b in blocks], axis=0)
        ordered[:, at : at + size] = jnp.dot(order, x, preferred_element_type=F32).astype(BF16)


def output_kernel(first, arrange, *refs):
    inputs, (keep_ref, send_ref) = refs[: -2 - bool(arrange)], refs[-2:]
    blocks, pieces = inputs[:-3], inputs[-3:]
    half, span = keep_ref.shape
    if arrange:
        ordered = refs[-3]
        arrange(*blocks, ordered)
    else:
        ordered = blocks[0]
    for at, size in chunks(span, 512):
        y, begin = 0.0, 0
        for piece in pieces:
            end = begin + piece.shape[0]
            y = y + jnp.dot(
                ordered[:, begin:end], piece[:, first + at : first + at + size], preferred_element_type=F32
            )
            begin = end
        keep_ref[:, at : at + size] = y[:half]
        send_ref[:, at : at + size] = y[half:].astype(BF16)


def pair_kernel(keep_ref, other_ref, *outs):
    block = outs[0].shape[0]
    for x, out in enumerate(outs):
        span = pl.ds(x * block, block)
        out[...] = (keep_ref[span] + other_ref[span].astype(F32)).astype(out.dtype)


def total_kernel(*refs):
    count = refs[-1].shape[1] // refs[0].shape[1]
    each = (len(refs) - 1) // count
    span = refs[0].shape[1]
    for i in range(count):
        part = refs[i * each : (i + 1) * each]
        refs[-1][:, i * span : (i + 1) * span] = sum(ref[...].astype(F32) for ref in part).astype(BF16)


def call(kernel, name, outs, inputs, scratch=(), specs=None, flops=0, size=0, exps=0):
    return pl.pallas_call(
        kernel,
        out_shape=outs,
        in_specs=specs or [whole()] * len(inputs),
        out_specs=jax.tree.map(lambda _: whole(), outs),
        scratch_shapes=list(scratch),
        compiler_params=params(),
        cost_estimate=pl.CostEstimate(flops=flops, bytes_accessed=size, transcendentals=exps),
        name=name,
    )(*inputs)


def body(hidden_in, norm_gain, qkv_weight, out_weight, lengths, key_cache, cache_of_values):
    wide = lax.axis_size("wide")
    narrow = lax.axis_size("narrow")
    steps, block_rows, depth = hidden_in.shape
    rows, kv_heads, slots, head_dim = key_cache.shape
    width = qkv_weight.shape[1]
    slice_width, out_width = out_weight.shape
    block = steps * block_rows
    tokens = block * wide
    per = steps * rows
    heads = slice_width * wide // head_dim
    shape = jax.ShapeDtypeStruct

    half = np.arange(head_dim) % (head_dim // 2)
    freqs = np.asarray(rope_base ** (-2.0 * half / head_dim), np.float32)[None]
    qkv_split = depth // 2
    ends = [slice_width // 8, slice_width * 3 // 8]

    (qkv_near,) = fetch([(qkv_weight, 0, qkv_split)], [])
    with jax.named_scope("gather_tokens"):
        own = hidden_in.reshape(block, depth)
        blocks = []
        for x in range(wide // 2):
            near = swap(own, "wide", 2 * x) if x else own
            if x:
                near, qkv_near = lax.optimization_barrier((near, qkv_near))
            blocks += [near, swap(near, "wide", 1)]
    partial = call(
        functools.partial(project_kernel, wide, narrow, steps, rows), "project",
        [shape((per * wide, LANES + width), BF16)] * narrow,
        blocks
        + [norm_gain.reshape(1, -1), resident(qkv_near), pltpu.with_memory_space_constraint(qkv_weight, pltpu.HBM)],
        [
            pltpu.VMEM((tokens, depth), BF16),
            pltpu.VMEM((tokens, width), F32),
            pltpu.VMEM((depth - qkv_split, width), BF16),
            pltpu.SemaphoreType.DMA((-(-(depth - qkv_split) // 512),)),
        ],
        [whole()] * (wide + 2) + [pl.BlockSpec(memory_space=pltpu.HBM)],
        flops=2 * tokens * depth * width, size=2 * depth * width,
    )
    keys, values, out_first, cosine, sine, mask = fetch(
        [(key_cache, 0, rows), (cache_of_values, 0, rows), (out_weight, 0, ends[0])],
        [partial[0]],
        (steps, lengths, jnp.asarray(freqs)),
    )
    with jax.named_scope("sum_over_narrow"):
        parts = [swap(partial[e], "narrow", e) if e else partial[e] for e in reversed(range(narrow))]
    normed = call(
        functools.partial(normalize_kernel, wide, narrow, depth * narrow), "normalize",
        [shape((per, width), BF16)] * wide,
        parts + [cosine],
        specs=[whole()] * narrow + [hbm()],
        size=4 * tokens * width,
    )
    (out_second,) = fetch([(out_weight, ends[0], ends[1] - ends[0])], [normed[0]])
    with jax.named_scope("columns_to_owner"):
        mine = [swap(p, "wide", d) if d else p for d, p in enumerate(normed)]
    common = [mask, cosine, sine, resident(keys), resident(values)]
    arrived, inputs, extra = {}, mine, [out_second]
    for low, span in ((wide // 2, wide // 2), (wide // 4, wide // 4), (0, wide // 4)):
        far = 2 * low == wide
        results = call(
            functools.partial(attend_kernel, wide, steps, slice_width, low, span), "attend",
            [shape((per, slice_width + LANES * far), BF16)] * span
            + ([shape((per, width * wide), F32)] if far else []),
            inputs + common + extra,
            ([pltpu.VMEM((wide, per, width), F32)] if far else [])
            + [
                pltpu.VMEM((kv_heads * span // wide, rows, steps * heads // kv_heads, head_dim), F32),
                pltpu.VMEM((span, per, slice_width), F32),
            ],
            [whole()] * (len(inputs) + 5) + [hbm()] * len(extra),
            flops=4 * per * heads * slots * head_dim * span // wide,
            size=4 * rows * kv_heads * slots * head_dim * span // wide,
            exps=per * heads * slots * span // wide,
        )
        with jax.named_scope("heads_to_weights"):
            for i in range(span):
                d = low + i
                arrived[d] = swap(results[i], "wide", d) if d else results[i]
        if far:
            inputs, extra = [results[-1]], []
    joined = call(
        functools.partial(join_kernel, list(arrived)), "join", shape((per * wide, slice_width), BF16),
        list(arrived.values()),
        [pltpu.VMEM((per * wide, slice_width), F32)], size=4 * per * wide * slice_width,
    )
    (out_last,) = fetch([(out_weight, ends[1], slice_width - ends[1])], [joined])
    with jax.named_scope("gather_over_narrow"):
        spread = [swap(joined, "narrow", e) if e else joined for e in reversed(range(narrow))]
    weights = [resident(out_first), resident(out_second), resident(out_last)]
    span = out_width // 2
    made = [shape((tokens // 2, span), F32), shape((tokens // 2, span), BF16)]
    arrange = functools.partial(arrange_kernel, wide, narrow, steps, rows)
    inputs, sums = spread, []
    for i in range(2):
        results = call(
            functools.partial(output_kernel, i * span, None if i else arrange), "output",
            ([] if i else [shape((tokens, slice_width), BF16)]) + made,
            inputs + weights,
            flops=2 * tokens * slice_width * span, size=2 * slice_width * span,
        )
        if not i:
            inputs, results = list(results[:1]), results[1:]
        keep, send = results
        with jax.named_scope("sum_over_wide"):
            other = swap(send, "wide", 1)
            chip = call(
                pair_kernel, "pair",
                [shape((block, span), BF16 if x else F32) for x in range(wide // 2)],
                [keep, other], size=6 * tokens * span // 2,
            )
            sums += [swap(c, "wide", 2 * x) if x else c for x, c in enumerate(chip)]
    total = call(
        total_kernel, "total", shape((block, out_width), BF16), sums, size=8 * block * out_width
    )
    return total.reshape(steps, block_rows, out_width)


def solution(mesh):
    in_specs = (
        P(None, ("groups", "wide"), "narrow"),
        P("narrow"),
        P("narrow", "wide"),
        P("wide", "narrow"),
        P(("groups", "wide", "narrow")),
        P(("groups", "wide", "narrow"), None, None, None),
        P(("groups", "wide", "narrow"), None, None, None),
    )
    out_specs = P(None, ("groups", "wide"), "narrow")
    return jax.shard_map(body, mesh=mesh, in_specs=in_specs, out_specs=out_specs, check_vma=False)
```
